512 devices in a mesh: section: 8 (over y), expert: 64 (over x, z, core).
Axes of the slice: x: 4, y: 8, z: 8, core: 2. Of those that a mesh axis runs over, the one named last changes fastest.
Arguments:
- section_input: bfloat16 [8, 6144, 2048], P('section', 'expert'), may hold values from -6 to 6
- saved_input: bfloat16 [8, 6144, 2048], P('section', 'expert'), may hold values from -6 to 6
- grad_input: bfloat16 [8, 6144, 2048], P('section', 'expert'), may hold values from -6 to 6
- expert_ids: int32 [8, 2, 6144, 2], P('section', None, 'expert'), may hold values from 0 to 15, all different within a row; in each aligned block of 96 rows (0 to 95, 96 to 191, ..., all dimensions but the last counted through in order) at most 16 rows name the same one
- keep_mask: int32 [8, 2, 6144, 2], P('section', None, 'expert'), may hold values 0 or 1
- norm_gain: float32 [8, 2048], P('section'), may hold values from 0.5 to 1.5
- router_weight: bfloat16 [8, 2048, 16], P('section'), may hold values from -0.25 to 0.25
- gate_weight: bfloat16 [8, 2048, 12288], P('section', None, 'expert'), may hold values from -0.125 to 0.125
- up_weight: bfloat16 [8, 2048, 12288], P('section', None, 'expert'), may hold values from -0.125 to 0.125
- down_weight: bfloat16 [8, 12288, 2048], P('section', 'expert'), may hold values from -0.21875 to 0.21875
Outputs:
- section_output: bfloat16 [8, 6144, 2048], P('section', 'expert')
- grad_output: bfloat16 [8, 6144, 2048], P('section', 'expert')
The draws below stay inside these ranges and needn't reach their ends.
Inputs may be any that keep to these rules, and one draw needn't show every extreme that they name: `expert_ids`: each token names 2 different experts. Among the 96 tokens that one index of expert holds for one section and micro-batch, no expert is named more than 16 times, a bound that some block reaches in some of them.
All inputs are finite; a program needn't handle non-finite values. No bound on the sum of `keep_mask` on one device may be relied on, other than what follows from the above.
Results may differ from the reference program's by a relative error of at most 0.012.
Values may be sent and summed in bfloat16 or wider, within the bound.
No kernel may reach another device: no remote copies, remote signals or barrier semaphores. Data moves between devices by JAX's collectives and lax.ppermute only.
A program may use at most 64 MiB of HBM per device.

```python
import math
import jax
import jax.numpy as jnp
import numpy as np
from jax import lax

D = 2048
H = 768
TOP = 2
TOK_MB = 96
SECTIONS = 8
EXPERTS = 16
TOKENS = 6144
MOST = 16
N_SECTION = 8
N_EXPERT = 64


def plant(values, own_key, low, top_value):
    spot = [jax.random.randint(jax.random.fold_in(own_key, axis), (), 0, length) for axis, length in enumerate(values.shape)]
    widest = values.shape.index(max(values.shape))
    neighbour = spot[:widest] + [(spot[widest] + 1) % values.shape[widest]] + spot[widest + 1:]
    return values.at[tuple(spot)].set(low).at[tuple(neighbour)].set(top_value)


def block_scale(stream_key, dims, cuts, smallest, top_value):
    factor_of = 1.0
    for axis_at, blocks in cuts:
        steps = jax.random.uniform(jax.random.fold_in(jax.random.fold_in(stream_key, 6), axis_at), (blocks,), jnp.float32, smallest / len(cuts), top_value / len(cuts))
        factor_of = factor_of * jnp.repeat(jnp.exp(steps), dims[axis_at] // blocks).reshape((-1,) + (1,) * (len(dims) - 1 - axis_at))
    return factor_of


def shared_out(rng, own, number, rows, count, top, reach, lean):
    order = jax.random.permutation(rng, count)
    heavy_load, usual = shares(count, rows * top, reach, lean, True), shares(count, rows * top, reach, lean, False)
    places = jnp.arange(count)

    def named(sizes, rotation):
        used = int((sizes > 0).sum())
        fixed = max(1, used // 4)
        shifted = fixed + (places - fixed + rotation * (used - fixed)) % max(1, count - fixed)
        return jnp.zeros((count,), jnp.int32).at[order[jnp.where(places < fixed, places, shifted)]].set(jnp.asarray(sizes, jnp.int32))

    sizes = jnp.where(number % 4 == 0, named(heavy_load, number // 4), named(usual, number - number // 4 - 1))
    mixed = jax.random.permutation(jax.random.fold_in(own, 3), count)
    source_of, receiver = mixed[0:count // 2 * 2:2], mixed[1:count // 2 * 2:2]
    margin = jnp.minimum(sizes[source_of] - 1, reach - sizes[receiver]) // 2
    margin = jnp.where((source_of == order[0]) | (receiver == order[0]) | (sizes[receiver] == 0), 0, jnp.maximum(margin, 0))
    shifted = jax.random.randint(jax.random.fold_in(own, 4), (count // 2,), 0, 1 << 20) % (margin + 1)
    sizes = sizes.at[source_of].add(-shifted).at[receiver].add(shifted)
    labels = jnp.searchsorted(jnp.cumsum(sizes), jnp.arange(rows * top), side="right").astype(jnp.int32)
    table = labels.reshape(top, rows).T
    table = table[jax.random.permutation(jax.random.fold_in(own, 1), rows)]
    rotation = jax.random.randint(jax.random.fold_in(own, 2), (rows, 1), 0, top)
    return jnp.take_along_axis(table, (jnp.arange(top)[None, :] + rotation) % top, axis=1)


def shares(number_of, total, bound, lean, full):
    weights = [(1 << 20) // math.isqrt(standing ** lean) + 1 for standing in range(1, number_of + 1)]
    largest = bound if full else min(bound, max(-(-total // number_of), total * weights[0] // sum(weights)))
    least = 1 if total - largest >= number_of - 1 else 0
    given, surplus = [largest] + [least] * (number_of - 1), total - largest - least * (number_of - 1)
    while surplus > 0:
        movable = [i for i in range(1, number_of) if given[i] < largest] or [i for i in range(1, number_of) if given[i] < bound]
        mass, budget = sum([weights[i] for i in movable]), surplus
        for i in movable:
            addition = min(bound - given[i], max(1, budget * weights[i] // mass), surplus)
            given[i] = given[i] + addition
            surplus = surplus - addition
    return np.array(given)


def gaussian(rng, extent, scale, bound, pieces=(), kind=jnp.bfloat16):
    values = jax.random.normal(rng, extent, jnp.float32) * scale
    if len(pieces) > 0:
        values = block_scale(rng, extent, pieces, -0.22, 0.18) * values
    return jnp.clip(values, min=-bound, max=bound).astype(kind)


def setup_inputs(seed: int = 0) -> dict:
    key_list = jax.random.split(jax.random.key(seed), 11)
    section_input = gaussian(key_list[0], (SECTIONS, TOKENS, D), 1.0, 6.0, ((0, 8), (1, 64)))
    saved_input = gaussian(key_list[1], (SECTIONS, TOKENS, D), 1.0, 6.0, ((0, 8), (1, 64)))
    grad_input = gaussian(key_list[2], (SECTIONS, TOKENS, D), 1.0, 6.0, ((0, 8), (1, 64)))
    expert_ids_keys = jax.random.split(jax.random.fold_in(key_list[3], 1), SECTIONS * 2 * TOKENS // TOK_MB)
    expert_ids_turns = jax.random.permutation(jax.random.fold_in(key_list[3], 3), SECTIONS * 2 * TOKENS // TOK_MB)
    expert_ids = jax.vmap(lambda own, number: shared_out(jax.random.fold_in(key_list[3], 2), own, number, TOK_MB, EXPERTS, TOP, MOST, 2))(expert_ids_keys, expert_ids_turns).reshape((SECTIONS, 2, TOKENS, TOP))
    keep_mask = plant((jax.random.randint(key_list[4], (SECTIONS, 2, TOKENS, TOP), 0, 8) < 7).astype(jnp.int32), jax.random.fold_in(key_list[4], 1), 0, 1)
    norm_gain = jnp.clip(0.5 + 1.0 * jax.random.uniform(key_list[5], (SECTIONS, D), jnp.float32) ** block_scale(key_list[5], (SECTIONS, D), ((0, 8),), -0.2, 0.2), 0.5, 1.5)
    router_weight = gaussian(key_list[6], (SECTIONS, D, EXPERTS), (D // 4) ** -0.5, 0.25, ((0, 8),))
    gate_weight = gaussian(key_list[7], (SECTIONS, D, EXPERTS * H), D ** -0.5, 0.125, ((0, 8), (2, 64)))
    up_weight = gaussian(key_list[8], (SECTIONS, D, EXPERTS * H), D ** -0.5, 0.125, ((0, 8), (2, 64)))
    down_weight = gaussian(key_list[9], (SECTIONS, EXPERTS * H, D), H ** -0.5, 0.21875, ((0, 8), (1, 64)))
    return {"section_input": section_input, "saved_input": saved_input, "grad_input": grad_input, "expert_ids": expert_ids, "keep_mask": keep_mask, "norm_gain": norm_gain, "router_weight": router_weight, "gate_weight": gate_weight, "up_weight": up_weight, "down_weight": down_weight}


EPS = 1e-06
KEEP_SCALE = 8.0 / 7.0

def normalize(hidden, gain_row):
    plain = hidden.astype(jnp.float32)
    inverse = lax.rsqrt(lax.optimization_barrier(jnp.mean(plain * plain, axis=-1, keepdims=True)) + EPS)
    return (plain, inverse, (plain * inverse * gain_row).astype(jnp.bfloat16))

def gating(normed, router_layer, chosen_ids, keep_bits):
    logits = jnp.dot(normed, router_layer, preferred_element_type=jnp.float32)
    picked = jnp.take_along_axis(logits, chosen_ids, axis=1)
    spread = jnp.exp(picked[:, None, :] - picked[:, :, None])
    gate_probs = 1.0 / lax.optimization_barrier(jnp.sum(spread, axis=2))
    return (gate_probs, keep_bits.astype(jnp.float32) * KEEP_SCALE * gate_probs)

def expert_forward(row_block, gate_full, up_full, down_full):
    pre_gate = jnp.dot(row_block, gate_full, preferred_element_type=jnp.float32)
    pre_up = jnp.dot(row_block, up_full, preferred_element_type=jnp.float32)
    inner_act = (pre_gate * jax.nn.sigmoid(pre_gate) * pre_up).astype(jnp.bfloat16)
    return jnp.dot(inner_act, down_full, preferred_element_type=jnp.float32).astype(jnp.bfloat16)

def expert_backward(row_block, upstream, gate_full, up_full, down_full):
    pre_gate = jnp.dot(row_block, gate_full, preferred_element_type=jnp.float32)
    pre_up = jnp.dot(row_block, up_full, preferred_element_type=jnp.float32)
    sigma_gate = jax.nn.sigmoid(pre_gate)
    inner_act = (pre_gate * sigma_gate * pre_up).astype(jnp.bfloat16)
    pulled = jnp.dot(upstream, down_full.T, preferred_element_type=jnp.float32)
    gate_change = lax.optimization_barrier(jnp.sum(inner_act.astype(jnp.float32) * pulled, axis=1)).astype(jnp.bfloat16)
    grad_gate = (pulled * pre_up * sigma_gate * (1.0 + pre_gate * (1.0 - sigma_gate))).astype(jnp.bfloat16)
    grad_up = (pulled * pre_gate * sigma_gate).astype(jnp.bfloat16)
    back_sum = jnp.dot(grad_gate, gate_full.T, preferred_element_type=jnp.float32)
    back_sum = back_sum + jnp.dot(grad_up, up_full.T, preferred_element_type=jnp.float32)
    return (back_sum.astype(jnp.bfloat16), gate_change)

def source_backward(plain, inverse, gain_row, router_layer, chosen_ids, keep_bits, gate_probs, scale, upstream, returned, gate_change):
    change = keep_bits.astype(jnp.float32) * KEEP_SCALE * gate_change.astype(jnp.float32)
    logit_grad = gate_probs * (change - lax.optimization_barrier(jnp.sum(gate_probs * change, axis=1, keepdims=True)))
    onehot = (chosen_ids[:, :, None] == jnp.arange(EXPERTS, dtype=jnp.int32)[None, None, :]).astype(jnp.float32)
    dense_grad = lax.optimization_barrier(jnp.sum(logit_grad[:, :, None] * onehot, axis=1))
    through_router = lax.dot_general(dense_grad, router_layer.astype(jnp.float32), (((1,), (1,)), ((), ())), precision=lax.Precision.HIGHEST, preferred_element_type=jnp.float32)
    total_grad = lax.optimization_barrier(jnp.sum(scale[:, :, None] * returned.astype(jnp.float32), axis=1)) + through_router
    weighted = total_grad * gain_row
    inner_mean = lax.optimization_barrier(jnp.mean(weighted * plain, axis=-1, keepdims=True))
    norm_grad = inverse * (weighted - plain * inverse * inverse * inner_mean)
    return (upstream.astype(jnp.float32) + norm_grad).astype(jnp.bfloat16)

def expert_block(gate_layer, up_layer, down_layer, expert):
    first_col = (expert * H).astype(jnp.int32)
    return (lax.dynamic_slice_in_dim(gate_layer, first_col, H, 1), lax.dynamic_slice_in_dim(up_layer, first_col, H, 1), lax.dynamic_slice_in_dim(down_layer, first_col, H, 0))

def by_expert(flat_ids, compute):
    count_all = flat_ids.shape[0]
    max_rows = min(N_EXPERT * MOST, count_all)
    sort_order = jnp.argsort(flat_ids, stable=True).astype(jnp.int32)
    counts = lax.optimization_barrier(jnp.sum((flat_ids[:, None] == jnp.arange(EXPERTS, dtype=jnp.int32)[None, :]).astype(jnp.int32), axis=0)).astype(jnp.int32)
    starts = (jnp.cumsum(counts) - counts).astype(jnp.int32)
    padded = jnp.concatenate([sort_order, jnp.full((max_rows,), count_all, jnp.int32)])

    def single(expert):
        picked_rows = lax.dynamic_slice(padded, (starts[expert],), (max_rows,))
        valid_rows = jnp.arange(max_rows, dtype=jnp.int32) < counts[expert]
        picked_rows = jnp.where(valid_rows, picked_rows, count_all).astype(jnp.int32)
        return (picked_rows, compute(expert, jnp.minimum(picked_rows, count_all - 1).astype(jnp.int32)))
    picked_all, results = lax.map(single, jnp.arange(EXPERTS, dtype=jnp.int32))
    flat_picks = picked_all.reshape(-1)

    def place_rows(values):
        tail_shape = values.shape[2:]
        table_rows = jnp.zeros((count_all + 1,) + tail_shape, values.dtype)
        return table_rows.at[flat_picks].set(values.reshape((-1,) + tail_shape))[:count_all]
    return jax.tree.map(place_rows, results)

def reference(section_input, saved_input, grad_input, expert_ids, keep_mask, norm_gain, router_weight, gate_weight, up_weight, down_weight):
    output_list = []
    grad_list = []
    for section_index in range(N_SECTION):
        gain_row = norm_gain[section_index]
        router_layer = router_weight[section_index]
        gate_layer = gate_weight[section_index]
        up_layer = up_weight[section_index]
        down_layer = down_weight[section_index]
        forward_ids = expert_ids[section_index, 0]
        backward_ids = expert_ids[section_index, 1]
        forward_plain, forward_inverse, forward_normed = normalize(section_input[section_index], gain_row)
        forward_probs, forward_scale = gating(forward_normed, router_layer, forward_ids, keep_mask[section_index, 0])

        def forward_rows(expert, picked_rows):
            gate_full, up_full, down_full = expert_block(gate_layer, up_layer, down_layer, expert)
            return expert_forward(forward_normed[picked_rows // TOP], gate_full, up_full, down_full)
        copies = by_expert(forward_ids.reshape(-1), forward_rows).reshape(TOKENS, TOP, D)
        mixed_out = forward_plain + lax.optimization_barrier(jnp.sum(forward_scale[:, :, None] * copies.astype(jnp.float32), axis=1))
        output_list.append(mixed_out.astype(jnp.bfloat16))
        backward_plain, backward_inverse, backward_normed = normalize(saved_input[section_index], gain_row)
        backward_probs, backward_scale = gating(backward_normed, router_layer, backward_ids, keep_mask[section_index, 1])
        upstream_all = grad_input[section_index]

        def backward_rows(expert, picked_rows):
            gate_full, up_full, down_full = expert_block(gate_layer, up_layer, down_layer, expert)
            owner_token = picked_rows // TOP
            return expert_backward(backward_normed[owner_token], upstream_all[owner_token], gate_full, up_full, down_full)
        returned_flat, change_flat = by_expert(backward_ids.reshape(-1), backward_rows)
        grad_list.append(source_backward(backward_plain, backward_inverse, gain_row, router_layer, backward_ids, keep_mask[section_index, 1], backward_probs, backward_scale, upstream_all, returned_flat.reshape(TOKENS, TOP, D), change_flat.reshape(TOKENS, TOP)))
    section_output = jnp.roll(jnp.stack(output_list), 1, axis=0)
    grad_output = jnp.roll(jnp.stack(grad_list), -1, axis=0)
    return (section_output, grad_output)
```

```python
import jax
import jax.numpy as jnp
from jax import lax
from jax.experimental import pallas as pl
from jax.experimental.pallas import tpu as pltpu
from jax.sharding import PartitionSpec as P

EPS = 1e-06
KEEP_SCALE = 8.0 / 7.0
NEAR_SETS = ((0, 2, 5, 7), (1, 3, 4, 6))
F32 = jnp.float32
BF16 = jnp.bfloat16
MIB = 1 << 20


def place(x, z, core):
    return (x * 8 + z) * 2 + core


def chips():
    return [(x, z, core) for x in range(4) for z in range(8) for core in range(2)]


def trade_groups():
    return [
        [place(x, z, core) for x in range(4) for z in zs]
        for zs in NEAR_SETS
        for core in range(2)
    ]


def z_partners():
    return [(place(x, z, c), place(x, z ^ 1, c)) for x, z, c in chips()]


def core_partners():
    return [(place(x, z, c), place(x, z, c ^ 1)) for x, z, c in chips()]


def shifted(block, distance):
    n = lax.axis_size("section")
    return lax.ppermute(block, "section", [((i - distance) % n, i) for i in range(n)])


def nt_dot(left, right):
    return lax.dot_general(
        left, right, (((1,), (1,)), ((), ())), preferred_element_type=F32
    )


def tn_dot(left, right):
    return lax.dot_general(
        left, right, (((0,), (0,)), ((), ())), preferred_element_type=F32
    )


def whole(shape):
    return pl.BlockSpec(shape, lambda *_: (0,) * len(shape))


def as_column(row):
    n = row.shape[1]
    eye = lax.broadcasted_iota(jnp.int32, (n, n), 0) == lax.broadcasted_iota(
        jnp.int32, (n, n), 1
    )
    return jnp.sum(jnp.where(eye, row, 0.0), axis=1, keepdims=True)


def prepare(hidden, gain, router_t, ids, keep, sel_ref, col_ref):
    tokens = hidden.shape[0]
    experts = router_t.shape[0]
    slots = sel_ref.shape[1]
    per = slots // experts
    plain = hidden.astype(F32)
    inverse = lax.rsqrt(jnp.mean(plain * plain, axis=-1, keepdims=True) + EPS)
    normed = (plain * inverse * gain).astype(BF16)
    logits = nt_dot(router_t, normed)
    expert_row = lax.broadcasted_iota(jnp.int32, (experts, tokens), 0)
    picked = [
        jnp.sum(jnp.where(expert_row == ids[k], logits, 0.0), axis=0, keepdims=True)
        for k in range(2)
    ]
    probs = [1.0 / (1.0 + jnp.exp(picked[1 - k] - picked[k])) for k in range(2)]
    slot = lax.broadcasted_iota(jnp.int32, (slots, tokens), 0)
    slot_expert = slot // per
    slot_rank = slot % per
    named = [slot_expert == ids[k] for k in range(2)]
    named_any = (named[0] | named[1]).astype(F32).astype(BF16)
    earlier = (
        lax.broadcasted_iota(jnp.int32, (tokens, tokens), 0)
        < lax.broadcasted_iota(jnp.int32, (tokens, tokens), 1)
    ).astype(F32).astype(BF16)
    rank = jnp.dot(named_any, earlier, preferred_element_type=F32)
    here = rank == slot_rank.astype(F32)
    sel = [(named[k] & here).astype(F32).astype(BF16) for k in range(2)]
    sel_ref[0] = sel[0]
    sel_ref[1] = sel[1]
    lane = lax.broadcasted_iota(jnp.int32, (tokens, 128), 1)
    kept = [keep[k].astype(F32) * KEEP_SCALE for k in range(2)]
    rows = [
        kept[0] * probs[0],
        kept[1] * probs[1],
        probs[0],
        probs[1],
        kept[0],
        kept[1],
        ids[0].astype(F32),
        ids[1].astype(F32),
    ]
    cols = jnp.zeros((tokens, 128), F32)
    for at, row in enumerate(rows):
        cols = jnp.where(lane == at, as_column(row), cols)
    col_ref[...] = jnp.where(lane == len(rows), inverse, cols)
    return normed, sel[0] + sel[1]


def prologue_kernel(
    fwd_ref, bwd_ref, up_ref, ids_ref, keep_ref, gain_ref, router_ref,
    send_ref, fsel_ref, fcol_ref, bsel_ref, bcol_ref,
):
    width = fwd_ref.shape[1]
    gain = gain_ref[...]
    router_t = router_ref[...]
    ids = [[ids_ref[m, k : k + 1, :] for k in range(2)] for m in range(2)]
    keep = [[keep_ref[m, k : k + 1, :] for k in range(2)] for m in range(2)]
    normed, sel = prepare(fwd_ref[...], gain, router_t, ids[0], keep[0], fsel_ref, fcol_ref)
    send_ref[:, :width] = jnp.dot(sel, normed, preferred_element_type=F32).astype(BF16)
    normed, sel = prepare(bwd_ref[...], gain, router_t, ids[1], keep[1], bsel_ref, bcol_ref)
    send_ref[:, width : 2 * width] = jnp.dot(
        sel, normed, preferred_element_type=F32
    ).astype(BF16)
    send_ref[:, 2 * width :] = jnp.dot(
        sel, up_ref[...], preferred_element_type=F32
    ).astype(BF16)


def prologue(fwd, bwd, upstream, ids, keep, gain, router_t, slots):
    tokens, width = fwd.shape
    sel = jax.ShapeDtypeStruct((2, slots, tokens), BF16)
    col = jax.ShapeDtypeStruct((tokens, 128), F32)
    outs = (jax.ShapeDtypeStruct((slots, 3 * width), BF16), sel, col, sel, col)
    args = (fwd, bwd, upstream, ids, keep, gain, router_t)
    return pl.pallas_call(
        prologue_kernel,
        out_shape=outs,
        grid=(1,),
        in_specs=[whole(a.shape) for a in args],
        out_specs=[whole(o.shape) for o in outs],
        compiler_params=pltpu.CompilerParams(vmem_limit_bytes=40 * MIB),
        cost_estimate=pl.CostEstimate(
            flops=6 * slots * tokens * width, bytes_accessed=5 * MIB, transcendentals=0
        ),
        name="prologue",
    )(*args)


def fetch(pieces, full, sems, first):
    rows = pieces[0].shape[0]
    copies = []
    for q, piece in enumerate(pieces):
        copy = pltpu.make_async_copy(
            piece, full.at[pl.ds(q * rows, rows)], sems.at[first + q]
        )
        copy.start()
        copies.append(copy)
    return copies


def forward_kernel(rows_ref, *rest):
    pieces = rest[:12]
    out_ref, gate, up, down, act, sems = rest[12:]
    gates = fetch(pieces[0:4], gate, sems, 0)
    ups = fetch(pieces[4:8], up, sems, 4)
    downs = fetch(pieces[8:12], down, sems, 8)
    rows = rows_ref[...]
    hidden = gate.shape[0]
    part = 256
    for at in range(0, hidden, part):
        for q in ((0, 1), (2,), (3,))[at // part]:
            gates[q].wait()
            ups[q].wait()
        pre_gate = nt_dot(rows, gate[at : at + part, :])
        pre_up = nt_dot(rows, up[at : at + part, :])
        act[:, at : at + part] = (
            pre_gate * jax.nn.sigmoid(pre_gate) * pre_up
        ).astype(BF16)
    for copy in downs:
        copy.wait()
    width = down.shape[1]
    step = 512
    for at in range(0, width, step):
        out_ref[:, at : at + step] = jnp.dot(
            act[...], down[:, at : at + step], preferred_element_type=F32
        ).astype(BF16)


def backward_kernel(rows_ref, upstream_ref, *rest):
    pieces = rest[:12]
    out_ref, gate, up, down, grad_gate, grad_up, sems = rest[12:]
    gates = fetch(pieces[0:4], gate, sems, 0)
    ups = fetch(pieces[4:8], up, sems, 4)
    downs = fetch(pieces[8:12], down, sems, 8)
    rows = rows_ref[...]
    upstream = upstream_ref[...]
    hidden = gate.shape[0]
    part = 256
    change = jnp.zeros((rows.shape[0], 1), F32)
    for at in range(0, hidden, part):
        for q in ((0, 1), (2,), (3,))[at // part]:
            gates[q].wait()
            ups[q].wait()
            downs[q].wait()
        pre_gate = nt_dot(rows, gate[at : at + part, :])
        pre_up = nt_dot(rows, up[at : at + part, :])
        pulled = nt_dot(upstream, down[at : at + part, :])
        sigma = jax.nn.sigmoid(pre_gate)
        inner = (pre_gate * sigma * pre_up).astype(BF16).astype(F32)
        change = change + jnp.sum(inner * pulled, axis=1, keepdims=True)
        grad_gate[:, at : at + part] = (
            pulled * pre_up * sigma * (1.0 + pre_gate * (1.0 - sigma))
        ).astype(BF16)
        grad_up[:, at : at + part] = (pulled * pre_gate * sigma).astype(BF16)
    width = gate.shape[1]
    step = 512
    for at in range(0, width, step):
        out_ref[:, at : at + step] = (
            jnp.dot(grad_gate[...], gate[:, at : at + step], preferred_element_type=F32)
            + jnp.dot(grad_up[...], up[:, at : at + step], preferred_element_type=F32)
        ).astype(BF16)
    out_ref[:, width:] = jnp.broadcast_to(change, (rows.shape[0], 128)).astype(BF16)


def expert_call(kernel, got, columns, extra, n_scratch, pieces, name):
    slots = got.shape[0]
    quarter, width = pieces[0].shape
    hidden = 4 * quarter
    full = pltpu.VMEM((hidden, width), BF16)
    return pl.pallas_call(
        kernel,
        out_shape=jax.ShapeDtypeStruct((slots, width + extra), BF16),
        grid=(1,),
        in_specs=[
            pl.BlockSpec((slots, width), lambda i, c=c: (0, c)) for c in columns
        ]
        + [pl.BlockSpec(memory_space=pltpu.HBM)] * 12,
        out_specs=whole((slots, width + extra)),
        scratch_shapes=[full, full, full]
        + [pltpu.VMEM((slots, hidden), BF16)] * n_scratch
        + [pltpu.SemaphoreType.DMA((12,))],
        compiler_params=pltpu.CompilerParams(vmem_limit_bytes=40 * MIB),
        cost_estimate=pl.CostEstimate(
            flops=2 * (2 * n_scratch + 1) * slots * width * hidden,
            bytes_accessed=12 * MIB,
            transcendentals=0,
        ),
        name=name,
    )(
        *[got for _ in columns],
        *[pltpu.with_memory_space_constraint(p, pltpu.HBM) for p in pieces],
    )


def forward_end_kernel(back_ref, sel_ref, col_ref, input_ref, out_ref):
    cols = col_ref[...]
    back = back_ref[...]
    mixed = cols[:, 0:1] * tn_dot(sel_ref[0], back)
    mixed = mixed + cols[:, 1:2] * tn_dot(sel_ref[1], back)
    out_ref[...] = (input_ref[...].astype(F32) + mixed).astype(BF16)


def backward_end_kernel(
    back_ref, sel_ref, col_ref, saved_ref, upstream_ref, gain_ref, router_ref, out_ref
):
    cols = col_ref[...]
    width = saved_ref.shape[1]
    experts = router_ref.shape[0]
    back = back_ref[:, :width]
    tail = back_ref[:, width:]
    change = [
        cols[:, 4 + k : 5 + k] * tn_dot(sel_ref[k], tail)[:, 0:1] for k in range(2)
    ]
    probs = [cols[:, 2 + k : 3 + k] for k in range(2)]
    centre = probs[0] * change[0] + probs[1] * change[1]
    lane = lax.broadcasted_iota(jnp.int32, (cols.shape[0], experts), 1).astype(F32)
    dense = jnp.zeros((cols.shape[0], experts), F32)
    for k in range(2):
        dense = dense + jnp.where(
            lane == cols[:, 6 + k : 7 + k], probs[k] * (change[k] - centre), 0.0
        )
    router_t = router_ref[...]
    total = jnp.zeros((cols.shape[0], width), F32)
    rest = dense
    for _ in range(3):
        term = rest.astype(BF16)
        rest = rest - term.astype(F32)
        total = total + jnp.dot(term, router_t, preferred_element_type=F32)
    for k in range(2):
        total = total + cols[:, k : k + 1] * tn_dot(sel_ref[k], back)
    plain = saved_ref[...].astype(F32)
    inverse = cols[:, 8:9]
    weighted = total * gain_ref[...]
    inner_mean = jnp.mean(weighted * plain, axis=-1, keepdims=True)
    norm_grad = inverse * (weighted - plain * inverse * inverse * inner_mean)
    out_ref[...] = (upstream_ref[...].astype(F32) + norm_grad).astype(BF16)


def end_call(kernel, args, like, name):
    return pl.pallas_call(
        kernel,
        out_shape=jax.ShapeDtypeStruct(like.shape, BF16),
        grid=(1,),
        in_specs=[whole(a.shape) for a in args],
        out_specs=whole(like.shape),
        compiler_params=pltpu.CompilerParams(vmem_limit_bytes=40 * MIB),
        cost_estimate=pl.CostEstimate(
            flops=4 * args[0].shape[0] * like.shape[0] * like.shape[1],
            bytes_accessed=3 * MIB,
            transcendentals=0,
        ),
        name=name,
    )(*args)


def trade(rows):
    groups = trade_groups()
    count = len(groups[0])
    blocks = rows.reshape(count, rows.shape[0] // count, rows.shape[1])
    blocks = lax.all_to_all(
        blocks, "expert", 0, 0, axis_index_groups=groups, tiled=True
    )
    return blocks.reshape(rows.shape)


def on_device(
    section_input,
    saved_input,
    grad_input,
    expert_ids,
    keep_mask,
    norm_gain,
    router_weight,
    gate_weight,
    up_weight,
    down_weight,
):
    own = (gate_weight[0].T, up_weight[0].T, down_weight[0])
    far = [lax.ppermute(w, "expert", z_partners()) for w in own]
    near = [lax.ppermute(w, "expert", core_partners()) for w in own]
    cross = [lax.ppermute(w, "expert", core_partners()) for w in far]
    pieces = [w for four in zip(own, near, far, cross) for w in four]
    ids = expert_ids[0].transpose(0, 2, 1)
    keep = keep_mask[0].transpose(0, 2, 1)
    router_t = router_weight[0].T
    experts = router_t.shape[0]
    slots = experts * 16
    send, fsel, fcol, bsel, bcol = prologue(
        section_input[0], saved_input[0], grad_input[0], ids, keep, norm_gain, router_t, slots
    )
    got = trade(send)
    out_f = expert_call(forward_kernel, got, (0,), 0, 1, pieces, "forward_rows")
    back_f = trade(out_f)
    out_b = expert_call(backward_kernel, got, (1, 2), 128, 2, pieces, "backward_rows")
    back_b = trade(out_b)
    mixed = end_call(
        forward_end_kernel, (back_f, fsel, fcol, section_input[0]), section_input[0], "forward_end"
    )
    input_grad = end_call(
        backward_end_kernel,
        (back_b, bsel, bcol, saved_input[0], grad_input[0], norm_gain, router_t),
        saved_input[0],
        "backward_end",
    )
    return (shifted(mixed, 1)[None], shifted(input_grad, -1)[None])


def solution(mesh):
    return jax.shard_map(
        on_device,
        mesh=mesh,
        in_specs=(
            P("section", "expert", None),
            P("section", "expert", None),
            P("section", "expert", None),
            P("section", None, "expert", None),
            P("section", None, "expert", None),
            P("section", None),
            P("section", None, None),
            P("section", None, "expert"),
            P("section", None, "expert"),
            P("section", "expert", None),
        ),
        out_specs=(P("section", "expert", None), P("section", "expert", None)),
        check_vma=False,
    )
```

```python
import functools

import jax
import jax.numpy as jnp
from jax import lax
from jax.experimental import pallas as pl
from jax.experimental.pallas import tpu as pltpu
from jax.sharding import PartitionSpec as P

EPS = 1e-06
KEEP_SCALE = 8.0 / 7.0
NEAR_SETS = ((0, 2, 5, 7), (1, 3, 4, 6))
F32 = jnp.float32
BF16 = jnp.bfloat16
MIB = 1 << 20


def place(x, z, core):
    return (x * 8 + z) * 2 + core


def chips():
    return [(x, z, core) for x in range(4) for z in range(8) for core in range(2)]


def trade_groups():
    return [
        [place(x, z, core) for x in range(4) for z in zs]
        for zs in NEAR_SETS
        for core in range(2)
    ]


def z_partners():
    return [(place(x, z, c), place(x, z ^ 1, c)) for x, z, c in chips()]


def core_partners():
    return [(place(x, z, c), place(x, z, c ^ 1)) for x, z, c in chips()]


def shifted(block, distance):
    n = lax.axis_size("section")
    return lax.ppermute(block, "section", [((i - distance) % n, i) for i in range(n)])


def nt_dot(left, right):
    return lax.dot_general(
        left, right, (((1,), (1,)), ((), ())), preferred_element_type=F32
    )


def tn_dot(left, right):
    return lax.dot_general(
        left, right, (((0,), (0,)), ((), ())), preferred_element_type=F32
    )


def whole(shape):
    return pl.BlockSpec(shape, lambda *_: (0,) * len(shape))


def as_column(row):
    n = row.shape[1]
    eye = lax.broadcasted_iota(jnp.int32, (n, n), 0) == lax.broadcasted_iota(
        jnp.int32, (n, n), 1
    )
    return jnp.sum(jnp.where(eye, row, 0.0), axis=1, keepdims=True)


def prepare(hidden, gain, router_t, ids, keep, sel_ref, col_ref):
    tokens = hidden.shape[0]
    experts = router_t.shape[0]
    slots = sel_ref.shape[1]
    per = slots // experts
    plain = hidden.astype(F32)
    inverse = lax.rsqrt(jnp.mean(plain * plain, axis=-1, keepdims=True) + EPS)
    normed = (plain * inverse * gain).astype(BF16)
    logits = nt_dot(router_t, normed)
    expert_row = lax.broadcasted_iota(jnp.int32, (experts, tokens), 0)
    picked = [
        jnp.sum(jnp.where(expert_row == ids[k], logits, 0.0), axis=0, keepdims=True)
        for k in range(2)
    ]
    probs = [1.0 / (1.0 + jnp.exp(picked[1 - k] - picked[k])) for k in range(2)]
    slot = lax.broadcasted_iota(jnp.int32, (slots, tokens), 0)
    slot_expert = slot // per
    slot_rank = slot % per
    named = [slot_expert == ids[k] for k in range(2)]
    named_any = (named[0] | named[1]).astype(F32).astype(BF16)
    earlier = (
        lax.broadcasted_iota(jnp.int32, (tokens, tokens), 0)
        < lax.broadcasted_iota(jnp.int32, (tokens, tokens), 1)
    ).astype(F32).astype(BF16)
    rank = jnp.dot(named_any, earlier, preferred_element_type=F32)
    here = rank == slot_rank.astype(F32)
    sel = [(named[k] & here).astype(F32).astype(BF16) for k in range(2)]
    sel_ref[0] = sel[0]
    sel_ref[1] = sel[1]
    lane = lax.broadcasted_iota(jnp.int32, (tokens, 128), 1)
    kept = [keep[k].astype(F32) * KEEP_SCALE for k in range(2)]
    rows = [
        kept[0] * probs[0],
        kept[1] * probs[1],
        probs[0],
        probs[1],
        kept[0],
        kept[1],
        ids[0].astype(F32),
        ids[1].astype(F32),
    ]
    cols = jnp.zeros((tokens, 128), F32)
    for at, row in enumerate(rows):
        cols = jnp.where(lane == at, as_column(row), cols)
    col_ref[...] = jnp.where(lane == len(rows), inverse, cols)
    return normed, sel[0] + sel[1]


def in_hbm(*arrays):
    return [pltpu.with_memory_space_constraint(a, pltpu.HBM) for a in arrays]


HBM_SPEC = pl.BlockSpec(memory_space=pltpu.HBM)


def start_copies(pairs, sems):
    copies = []
    for at, (source, target) in enumerate(pairs):
        copy = pltpu.make_async_copy(source, target, sems.at[at])
        copy.start()
        copies.append(copy)
    return copies


def prologue_kernel(
    fwd_hbm, bwd_hbm, up_hbm, ids_hbm, keep_hbm, gain_hbm, router_hbm,
    send_hbm, fsel_ref, fcol_ref, bsel_ref, bcol_ref,
    fwd_ref, bwd_ref, up_ref, ids_ref, keep_ref, gain_ref, router_ref, send_ref, sems,
):
    width = fwd_ref.shape[1]
    loads = start_copies(
        [
            (gain_hbm, gain_ref),
            (router_hbm, router_ref),
            (ids_hbm, ids_ref),
            (keep_hbm, keep_ref),
            (fwd_hbm, fwd_ref),
            (bwd_hbm, bwd_ref),
            (up_hbm, up_ref),
        ],
        sems,
    )
    for load in loads[:5]:
        load.wait()
    gain = gain_ref[...]
    router_t = router_ref[...]
    ids = [[ids_ref[m, k : k + 1, :] for k in range(2)] for m in range(2)]
    keep = [[keep_ref[m, k : k + 1, :] for k in range(2)] for m in range(2)]
    stores = []

    def put(place, sel, values):
        part = pl.ds(place * width, width)
        send_ref[:, part] = jnp.dot(sel, values, preferred_element_type=F32).astype(BF16)
        store = pltpu.make_async_copy(
            send_ref.at[:, part], send_hbm.at[:, part], sems.at[7 + place]
        )
        store.start()
        stores.append(store)

    normed, sel = prepare(fwd_ref[...], gain, router_t, ids[0], keep[0], fsel_ref, fcol_ref)
    put(0, sel, normed)
    loads[5].wait()
    normed, sel = prepare(bwd_ref[...], gain, router_t, ids[1], keep[1], bsel_ref, bcol_ref)
    put(1, sel, normed)
    loads[6].wait()
    put(2, sel, up_ref[...])
    for store in stores:
        store.wait()


def prologue(fwd, bwd, upstream, ids, keep, gain, router_t, slots):
    tokens, width = fwd.shape
    sel = jax.ShapeDtypeStruct((2, slots, tokens), BF16)
    col = jax.ShapeDtypeStruct((tokens, 128), F32)
    vmem = pl.BlockSpec(memory_space=pltpu.VMEM)
    args = (fwd, bwd, upstream, ids, keep, gain, router_t)
    return pl.pallas_call(
        prologue_kernel,
        out_shape=(pltpu.HBM((slots, 3 * width), BF16), sel, col, sel, col),
        in_specs=[HBM_SPEC] * len(args),
        out_specs=[HBM_SPEC] + [vmem] * 4,
        scratch_shapes=[pltpu.VMEM(a.shape, a.dtype) for a in args]
        + [pltpu.VMEM((slots, 3 * width), BF16), pltpu.SemaphoreType.DMA((10,))],
        compiler_params=pltpu.CompilerParams(vmem_limit_bytes=24 * MIB),
        cost_estimate=pl.CostEstimate(
            flops=6 * slots * tokens * width, bytes_accessed=5 * MIB, transcendentals=0
        ),
        name="prologue",
    )(*in_hbm(*args))


def load_pieces(pieces, full, n_pieces):
    quarter = pieces[0].shape[0]
    return [
        (piece, full.at[pl.ds((at % n_pieces) * quarter, quarter)])
        for at, piece in enumerate(pieces)
    ]


def gate_terms(pre_gate, pre_up):
    sigma = jax.nn.sigmoid(pre_gate)
    inner = (pre_gate * sigma * pre_up).astype(BF16)
    to_gate = pre_up * sigma * (1.0 + pre_gate * (1.0 - sigma))
    return inner, to_gate, pre_gate * sigma


STEP = 512


def near_kernel(n, *refs):
    got_hbm, pieces, refs = refs[0], refs[1 : 1 + 3 * n], refs[1 + 3 * n :]
    sum_f, sum_b, change_ref, got, gate, up, down, sems = refs
    width = gate.shape[1]
    pairs = [(got_hbm, got)]
    pairs += load_pieces(pieces[:n], gate, n)
    pairs += load_pieces(pieces[n : 2 * n], up, n)
    pairs += load_pieces(pieces[2 * n :], down, n)
    copies = start_copies(pairs, sems)
    for copy in copies[: 1 + 2 * n]:
        copy.wait()
    rows = got[:, :width]
    act, _, _ = gate_terms(nt_dot(rows, gate[...]), nt_dot(rows, up[...]))
    for copy in copies[1 + 2 * n :]:
        copy.wait()
    for at in range(0, width, STEP):
        sum_f[:, at : at + STEP] = jnp.dot(
            act, down[:, at : at + STEP], preferred_element_type=F32
        )
    rows = got[:, width : 2 * width]
    inner, to_gate, to_up = gate_terms(nt_dot(rows, gate[...]), nt_dot(rows, up[...]))
    pulled = nt_dot(got[:, 2 * width :], down[...])
    change = jnp.sum(inner.astype(F32) * pulled, axis=1, keepdims=True)
    change_ref[...] = jnp.broadcast_to(change, change_ref.shape)
    grad_gate = (pulled * to_gate).astype(BF16)
    grad_up = (pulled * to_up).astype(BF16)
    for at in range(0, width, STEP):
        sum_b[:, at : at + STEP] = jnp.dot(
            grad_gate, gate[:, at : at + STEP], preferred_element_type=F32
        ) + jnp.dot(grad_up, up[:, at : at + STEP], preferred_element_type=F32)


def front_kernel(n, *refs):
    got_hbm, pieces, refs = refs[0], refs[1 : 1 + 2 * n], refs[1 + 2 * n :]
    act_ref, inner_ref, to_gate_ref, to_up_ref, got, gate, up, sems = refs
    width = gate.shape[1]
    pairs = [(got_hbm.at[:, pl.ds(0, 2 * width)], got)]
    pairs += load_pieces(pieces[:n], gate, n)
    pairs += load_pieces(pieces[n:], up, n)
    for copy in start_copies(pairs, sems):
        copy.wait()
    rows = got[:, :width]
    act, _, _ = gate_terms(nt_dot(rows, gate[...]), nt_dot(rows, up[...]))
    act_ref[...] = act
    rows = got[:, width:]
    inner, to_gate, to_up = gate_terms(nt_dot(rows, gate[...]), nt_dot(rows, up[...]))
    inner_ref[...] = inner
    to_gate_ref[...] = to_gate
    to_up_ref[...] = to_up


def far_kernel(n, *refs):
    got_hbm, pieces, refs = refs[0], refs[1 : 1 + 3 * n], refs[1 + 3 * n :]
    sum_f, sum_b, change_ref, act, inner, to_gate, to_up, out_hbm = refs[:8]
    upstream, gate, up, down, out, sems = refs[8:]
    width = gate.shape[1]
    pairs = load_pieces(pieces[2 * n :], down, n)
    pairs += [(got_hbm.at[:, pl.ds(2 * width, width)], upstream)]
    pairs += load_pieces(pieces[:n], gate, n)
    pairs += load_pieces(pieces[n : 2 * n], up, n)
    copies = start_copies(pairs, sems)
    stores = []

    def store(at, size):
        part = pl.ds(at, size)
        copy = pltpu.make_async_copy(
            out.at[:, part], out_hbm.at[:, part], sems.at[len(pairs) + len(stores)]
        )
        copy.start()
        stores.append(copy)

    for copy in copies[: n + 1]:
        copy.wait()
    pulled = nt_dot(upstream[...], down[...])
    change = jnp.sum(inner[...].astype(F32) * pulled, axis=1, keepdims=True)
    out[:, 2 * width :] = (change_ref[...] + change).astype(BF16)
    grad_gate = (pulled * to_gate[...]).astype(BF16)
    grad_up = (pulled * to_up[...]).astype(BF16)
    for at in range(0, width, STEP):
        out[:, at : at + STEP] = (
            sum_f[:, at : at + STEP]
            + jnp.dot(act[...], down[:, at : at + STEP], preferred_element_type=F32)
        ).astype(BF16)
    store(0, width)
    for copy in copies[n + 1 :]:
        copy.wait()
    for at in range(0, width, STEP):
        out[:, width + at : width + at + STEP] = (
            sum_b[:, at : at + STEP]
            + jnp.dot(grad_gate, gate[:, at : at + STEP], preferred_element_type=F32)
            + jnp.dot(grad_up, up[:, at : at + STEP], preferred_element_type=F32)
        ).astype(BF16)
    store(width, width + 128)
    for copy in stores:
        copy.wait()


def expert_calls(got, near_pieces, far_pieces, after_near):
    slots = got.shape[0]
    n = 2
    quarter, width = near_pieces[0].shape
    hidden = n * quarter
    full = pltpu.VMEM((hidden, width), BF16)
    vmem = pl.BlockSpec(memory_space=pltpu.VMEM)
    anywhere = pl.BlockSpec(memory_space=pl.ANY)

    def shape(columns, dtype):
        return jax.ShapeDtypeStruct((slots, columns), dtype)

    def params(dots, mib):
        return dict(
            compiler_params=pltpu.CompilerParams(vmem_limit_bytes=mib * MIB),
            cost_estimate=pl.CostEstimate(
                flops=2 * dots * slots * width * hidden,
                bytes_accessed=8 * MIB,
                transcendentals=0,
            ),
        )

    sums = pl.pallas_call(
        functools.partial(near_kernel, n),
        out_shape=[shape(width, F32), shape(width, F32), shape(128, F32)],
        in_specs=[anywhere] + [HBM_SPEC] * 6,
        out_specs=[vmem] * 3,
        scratch_shapes=[pltpu.VMEM(got.shape, BF16), full, full, full]
        + [pltpu.SemaphoreType.DMA((7,))],
        name="near_share",
        **params(8, 32),
    )(got, *near_pieces)
    far_pieces, sums = after_near(far_pieces, sums)
    fronts = pl.pallas_call(
        functools.partial(front_kernel, n),
        out_shape=[
            shape(hidden, BF16),
            shape(hidden, BF16),
            shape(hidden, F32),
            shape(hidden, F32),
        ],
        in_specs=[anywhere] + [HBM_SPEC, anywhere] * 2,
        out_specs=[vmem] * 4,
        scratch_shapes=[pltpu.VMEM((slots, 2 * width), BF16), full, full]
        + [pltpu.SemaphoreType.DMA((5,))],
        name="far_front",
        **params(4, 24),
    )(got, *far_pieces[:4])
    return pl.pallas_call(
        functools.partial(far_kernel, n),
        out_shape=pltpu.HBM((slots, 2 * width + 128), BF16),
        in_specs=[anywhere] + [HBM_SPEC, anywhere] * 3 + [vmem] * 7,
        out_specs=HBM_SPEC,
        scratch_shapes=[pltpu.VMEM((slots, width), BF16), full, full, full]
        + [pltpu.VMEM((slots, 2 * width + 128), BF16)]
        + [pltpu.SemaphoreType.DMA((9,))],
        name="far_rest",
        **params(4, 32),
    )(got, *far_pieces, *sums, *fronts)


def forward_end_kernel(back_ref, sel_ref, col_ref, input_ref, out_ref):
    cols = col_ref[...]
    back = back_ref[:, : input_ref.shape[1]]
    mixed = cols[:, 0:1] * tn_dot(sel_ref[0], back)
    mixed = mixed + cols[:, 1:2] * tn_dot(sel_ref[1], back)
    out_ref[...] = (input_ref[...].astype(F32) + mixed).astype(BF16)


def backward_end_kernel(
    back_ref, sel_ref, col_ref, saved_ref, upstream_ref, gain_ref, router_ref, out_ref
):
    cols = col_ref[...]
    width = saved_ref.shape[1]
    experts = router_ref.shape[0]
    back = back_ref[:, width : 2 * width]
    tail = back_ref[:, 2 * width :]
    change = [
        cols[:, 4 + k : 5 + k] * tn_dot(sel_ref[k], tail)[:, 0:1] for k in range(2)
    ]
    probs = [cols[:, 2 + k : 3 + k] for k in range(2)]
    centre = probs[0] * change[0] + probs[1] * change[1]
    lane = lax.broadcasted_iota(jnp.int32, (cols.shape[0], experts), 1).astype(F32)
    dense = jnp.zeros((cols.shape[0], experts), F32)
    for k in range(2):
        dense = dense + jnp.where(
            lane == cols[:, 6 + k : 7 + k], probs[k] * (change[k] - centre), 0.0
        )
    router_t = router_ref[...]
    total = jnp.zeros((cols.shape[0], width), F32)
    rest = dense
    for _ in range(3):
        term = rest.astype(BF16)
        rest = rest - term.astype(F32)
        total = total + jnp.dot(term, router_t, preferred_element_type=F32)
    for k in range(2):
        total = total + cols[:, k : k + 1] * tn_dot(sel_ref[k], back)
    plain = saved_ref[...].astype(F32)
    inverse = cols[:, 8:9]
    weighted = total * gain_ref[...]
    inner_mean = jnp.mean(weighted * plain, axis=-1, keepdims=True)
    norm_grad = inverse * (weighted - plain * inverse * inverse * inner_mean)
    out_ref[...] = (upstream_ref[...].astype(F32) + norm_grad).astype(BF16)


def end_call(kernel, args, like, name):
    return pl.pallas_call(
        kernel,
        out_shape=jax.ShapeDtypeStruct(like.shape, BF16),
        grid=(1,),
        in_specs=[whole(a.shape) for a in args],
        out_specs=whole(like.shape),
        compiler_params=pltpu.CompilerParams(vmem_limit_bytes=40 * MIB),
        cost_estimate=pl.CostEstimate(
            flops=4 * args[0].shape[0] * like.shape[0] * like.shape[1],
            bytes_accessed=3 * MIB,
            transcendentals=0,
        ),
        name=name,
    )(*args)


def trade(rows):
    groups = trade_groups()
    count = len(groups[0])
    blocks = rows.reshape(count, rows.shape[0] // count, rows.shape[1])
    blocks = lax.all_to_all(
        blocks, "expert", 0, 0, axis_index_groups=groups, tiled=True
    )
    return blocks.reshape(rows.shape)


def paired(held, passed):
    return [w for h, p in zip(held, passed) for w in (*in_hbm(h), p)]


def on_device(
    section_input,
    saved_input,
    grad_input,
    expert_ids,
    keep_mask,
    norm_gain,
    router_weight,
    gate_weight,
    up_weight,
    down_weight,
):
    own = (gate_weight[0].T, up_weight[0].T, down_weight[0])
    across, between = z_partners(), core_partners()
    far = [lax.ppermute(w, "expert", across) for w in own]
    near = in_hbm(*[lax.ppermute(w, "expert", between) for w in own])
    ids = expert_ids[0].transpose(0, 2, 1)
    keep = keep_mask[0].transpose(0, 2, 1)
    router_t = router_weight[0].T
    slots = router_t.shape[0] * 16
    send, fsel, fcol, bsel, bcol = prologue(
        section_input[0], saved_input[0], grad_input[0], ids, keep, norm_gain, router_t, slots
    )
    send, far[0] = lax.optimization_barrier((send, far[0]))
    got = trade(send)

    def cross(pieces, sums):
        late, sums = lax.optimization_barrier((pieces[1:], sums))
        pieces = [pieces[0], *late]
        crossed = [lax.ppermute(w, "expert", between) for w in pieces]
        return paired(pieces, crossed), sums

    out = expert_calls(got, paired(own, near), far, cross)
    back = trade(out)
    mixed = end_call(
        forward_end_kernel, (back, fsel, fcol, section_input[0]), section_input[0], "forward_end"
    )
    input_grad = end_call(
        backward_end_kernel,
        (back, bsel, bcol, saved_input[0], grad_input[0], norm_gain, router_t),
        saved_input[0],
        "backward_end",
    )
    return (shifted(mixed[None], 1), shifted(input_grad[None], -1))


def solution(mesh):
    return jax.shard_map(
        on_device,
        mesh=mesh,
        in_specs=(
            P("section", "expert", None),
            P("section", "expert", None),
            P("section", "expert", None),
            P("section", None, "expert", None),
            P("section", None, "expert", None),
            P("section", None),
            P("section", None, None),
            P("section", None, "expert"),
            P("section", None, "expert"),
            P("section", "expert", None),
        ),
        out_specs=(P("section", "expert", None), P("section", "expert", None)),
        check_vma=False,
    )
```

```python
import functools

import jax
import jax.numpy as jnp
from jax import lax
from jax.experimental import pallas as pl
from jax.experimental.pallas import tpu as pltpu
from jax.sharding import PartitionSpec as P

EPS = 1e-06
KEEP_SCALE = 8.0 / 7.0
NEAR_SETS = ((0, 2, 5, 7), (1, 3, 4, 6))
F32 = jnp.float32
BF16 = jnp.bfloat16
MIB = 1 << 20


def place(x, z, core):
    return (x * 8 + z) * 2 + core


def chips():
    return [(x, z, core) for x in range(4) for z in range(8) for core in range(2)]


def trade_groups():
    return [
        [place(x, z, core) for x in range(4) for z in zs]
        for zs in NEAR_SETS
        for core in range(2)
    ]


def z_partners():
    return [(place(x, z, c), place(x, z ^ 1, c)) for x, z, c in chips()]


def core_partners():
    return [(place(x, z, c), place(x, z, c ^ 1)) for x, z, c in chips()]


def shifted(block, distance):
    n = lax.axis_size("section")
    return lax.ppermute(block, "section", [((i - distance) % n, i) for i in range(n)])


def nt_dot(left, right):
    return lax.dot_general(
        left, right, (((1,), (1,)), ((), ())), preferred_element_type=F32
    )


def tn_dot(left, right):
    return lax.dot_general(
        left, right, (((0,), (0,)), ((), ())), preferred_element_type=F32
    )


def whole(shape):
    return pl.BlockSpec(shape, lambda *_: (0,) * len(shape))


def as_column(row):
    n = row.shape[1]
    eye = lax.broadcasted_iota(jnp.int32, (n, n), 0) == lax.broadcasted_iota(
        jnp.int32, (n, n), 1
    )
    return jnp.sum(jnp.where(eye, row, 0.0), axis=1, keepdims=True)


def prepare(hidden, gain, router_t, ids, keep, sel_ref, col_ref):
    tokens = hidden.shape[0]
    experts = router_t.shape[0]
    slots = sel_ref.shape[1]
    per = slots // experts
    plain = hidden.astype(F32)
    inverse = lax.rsqrt(jnp.mean(plain * plain, axis=-1, keepdims=True) + EPS)
    normed = (plain * inverse * gain).astype(BF16)
    logits = nt_dot(router_t, normed)
    expert_row = lax.broadcasted_iota(jnp.int32, (experts, tokens), 0)
    picked = [
        jnp.sum(jnp.where(expert_row == ids[k], logits, 0.0), axis=0, keepdims=True)
        for k in range(2)
    ]
    probs = [1.0 / (1.0 + jnp.exp(picked[1 - k] - picked[k])) for k in range(2)]
    slot = lax.broadcasted_iota(jnp.int32, (slots, tokens), 0)
    slot_expert = slot // per
    slot_rank = slot % per
    named = [slot_expert == ids[k] for k in range(2)]
    named_any = (named[0] | named[1]).astype(F32).astype(BF16)
    earlier = (
        lax.broadcasted_iota(jnp.int32, (tokens, tokens), 0)
        < lax.broadcasted_iota(jnp.int32, (tokens, tokens), 1)
    ).astype(F32).astype(BF16)
    rank = jnp.dot(named_any, earlier, preferred_element_type=F32)
    here = rank == slot_rank.astype(F32)
    sel = [(named[k] & here).astype(F32).astype(BF16) for k in range(2)]
    sel_ref[0] = sel[0]
    sel_ref[1] = sel[1]
    lane = lax.broadcasted_iota(jnp.int32, (tokens, 128), 1)
    kept = [keep[k].astype(F32) * KEEP_SCALE for k in range(2)]
    rows = [
        kept[0] * probs[0],
        kept[1] * probs[1],
        probs[0],
        probs[1],
        kept[0],
        kept[1],
        ids[0].astype(F32),
        ids[1].astype(F32),
    ]
    cols = jnp.zeros((tokens, 128), F32)
    for at, row in enumerate(rows):
        cols = jnp.where(lane == at, as_column(row), cols)
    col_ref[...] = jnp.where(lane == len(rows), inverse, cols)
    return normed, sel[0] + sel[1]


def in_hbm(*arrays):
    return [pltpu.with_memory_space_constraint(a, pltpu.HBM) for a in arrays]


HBM_SPEC = pl.BlockSpec(memory_space=pltpu.HBM)


def start_copies(pairs, sems):
    copies = []
    for at, (source, target) in enumerate(pairs):
        copy = pltpu.make_async_copy(source, target, sems.at[at])
        copy.start()
        copies.append(copy)
    return copies


def prologue_kernel(
    fwd_hbm, bwd_hbm, up_hbm, ids_hbm, keep_hbm, gain_hbm, router_hbm,
    send_hbm, fsel_ref, fcol_ref, bsel_ref, bcol_ref,
    fwd_ref, bwd_ref, up_ref, ids_ref, keep_ref, gain_ref, router_ref, send_ref, sems,
):
    width = fwd_ref.shape[1]
    loads = start_copies(
        [
            (gain_hbm, gain_ref),
            (router_hbm, router_ref),
            (ids_hbm, ids_ref),
            (keep_hbm, keep_ref),
            (fwd_hbm, fwd_ref),
            (bwd_hbm, bwd_ref),
            (up_hbm, up_ref),
        ],
        sems,
    )
    for load in loads[:5]:
        load.wait()
    gain = gain_ref[...]
    router_t = router_ref[...]
    ids = [[ids_ref[m, k : k + 1, :] for k in range(2)] for m in range(2)]
    keep = [[keep_ref[m, k : k + 1, :] for k in range(2)] for m in range(2)]
    stores = []

    def put(place, sel, values):
        part = pl.ds(place * width, width)
        send_ref[:, part] = jnp.dot(sel, values, preferred_element_type=F32).astype(BF16)
        store = pltpu.make_async_copy(
            send_ref.at[:, part], send_hbm.at[:, part], sems.at[7 + place]
        )
        store.start()
        stores.append(store)

    normed, sel = prepare(fwd_ref[...], gain, router_t, ids[0], keep[0], fsel_ref, fcol_ref)
    put(0, sel, normed)
    loads[5].wait()
    normed, sel = prepare(bwd_ref[...], gain, router_t, ids[1], keep[1], bsel_ref, bcol_ref)
    put(1, sel, normed)
    loads[6].wait()
    put(2, sel, up_ref[...])
    for store in stores:
        store.wait()


def prologue(fwd, bwd, upstream, ids, keep, gain, router_t, slots):
    tokens, width = fwd.shape
    sel = jax.ShapeDtypeStruct((2, slots, tokens), BF16)
    col = jax.ShapeDtypeStruct((tokens, 128), F32)
    vmem = pl.BlockSpec(memory_space=pltpu.VMEM)
    args = (fwd, bwd, upstream, ids, keep, gain, router_t)
    return pl.pallas_call(
        prologue_kernel,
        out_shape=(pltpu.HBM((slots, 3 * width), BF16), sel, col, sel, col),
        in_specs=[HBM_SPEC] * len(args),
        out_specs=[HBM_SPEC] + [vmem] * 4,
        scratch_shapes=[pltpu.VMEM(a.shape, a.dtype) for a in args]
        + [pltpu.VMEM((slots, 3 * width), BF16), pltpu.SemaphoreType.DMA((10,))],
        compiler_params=pltpu.CompilerParams(vmem_limit_bytes=24 * MIB),
        cost_estimate=pl.CostEstimate(
            flops=6 * slots * tokens * width, bytes_accessed=5 * MIB, transcendentals=0
        ),
        name="prologue",
    )(*in_hbm(*args))


def load_pieces(pieces, full, n_pieces):
    quarter = pieces[0].shape[0]
    return [
        (piece, full.at[pl.ds((at % n_pieces) * quarter, quarter)])
        for at, piece in enumerate(pieces)
    ]


def gate_terms(pre_gate, pre_up):
    sigma = jax.nn.sigmoid(pre_gate)
    inner = (pre_gate * sigma * pre_up).astype(BF16)
    to_gate = pre_up * sigma * (1.0 + pre_gate * (1.0 - sigma))
    return inner, to_gate, pre_gate * sigma


STEP = 512


def row_loads(got_hbm, rows, batches):
    slots = got_hbm.shape[0]
    width = rows.shape[1]
    return [
        (got_hbm.at[:, pl.ds(m * width, width)], rows.at[pl.ds(m * slots, slots)])
        for m in range(batches)
    ]


def near_kernel(n, *refs):
    got_hbm, pieces, refs = refs[0], refs[1 : 1 + 3 * n], refs[1 + 3 * n :]
    sum_f, sum_b, change_ref, rows, gate, up, down, sems = refs
    width = gate.shape[1]
    slots = sum_f.shape[0]
    row_pairs = row_loads(got_hbm, rows, 3)
    pairs = row_pairs[:2] + load_pieces(pieces[:n], gate, n)
    pairs += load_pieces(pieces[n : 2 * n], up, n)
    pairs += row_pairs[2:] + load_pieces(pieces[2 * n :], down, n)
    copies = start_copies(pairs, sems)
    for copy in copies[: 2 + n]:
        copy.wait()
    both = rows[: 2 * slots, :]
    pre_gate = nt_dot(both, gate[...])
    for copy in copies[2 + n : 2 + 2 * n]:
        copy.wait()
    pre_up = nt_dot(both, up[...])
    act, _, _ = gate_terms(pre_gate[:slots], pre_up[:slots])
    inner, to_gate, to_up = gate_terms(pre_gate[slots:], pre_up[slots:])
    for copy in copies[2 + 2 * n :]:
        copy.wait()
    for at in range(0, width, STEP):
        sum_f[:, at : at + STEP] = jnp.dot(
            act, down[:, at : at + STEP], preferred_element_type=F32
        )
    pulled = nt_dot(rows[2 * slots :, :], down[...])
    change = jnp.sum(inner.astype(F32) * pulled, axis=1, keepdims=True)
    change_ref[...] = jnp.broadcast_to(change, change_ref.shape)
    grad_gate = (pulled * to_gate).astype(BF16)
    grad_up = (pulled * to_up).astype(BF16)
    for at in range(0, width, STEP):
        sum_b[:, at : at + STEP] = jnp.dot(
            grad_gate, gate[:, at : at + STEP], preferred_element_type=F32
        ) + jnp.dot(grad_up, up[:, at : at + STEP], preferred_element_type=F32)


def front_kernel(n, *refs):
    got_hbm, pieces, refs = refs[0], refs[1 : 1 + 2 * n], refs[1 + 2 * n :]
    act_ref, inner_ref, to_gate_ref, to_up_ref, rows, gate, up, sems = refs
    slots = act_ref.shape[0]
    pairs = row_loads(got_hbm, rows, 2) + load_pieces(pieces[:n], gate, n)
    pairs += load_pieces(pieces[n:], up, n)
    copies = start_copies(pairs, sems)
    for copy in copies[: 2 + n]:
        copy.wait()
    pre_gate = nt_dot(rows[...], gate[...])
    for copy in copies[2 + n :]:
        copy.wait()
    pre_up = nt_dot(rows[...], up[...])
    act, _, _ = gate_terms(pre_gate[:slots], pre_up[:slots])
    act_ref[...] = act
    inner, to_gate, to_up = gate_terms(pre_gate[slots:], pre_up[slots:])
    inner_ref[...] = inner
    to_gate_ref[...] = to_gate
    to_up_ref[...] = to_up


def far_kernel(n, *refs):
    got_hbm, pieces, refs = refs[0], refs[1 : 1 + 3 * n], refs[1 + 3 * n :]
    sum_f, sum_b, change_ref, act, inner, to_gate, to_up, out_hbm = refs[:8]
    upstream, gate, up, down, out, sems = refs[8:]
    width = gate.shape[1]
    pairs = load_pieces(pieces[2 * n :], down, n)
    pairs += [(got_hbm.at[:, pl.ds(2 * width, width)], upstream)]
    pairs += load_pieces(pieces[:n], gate, n)
    pairs += load_pieces(pieces[n : 2 * n], up, n)
    copies = start_copies(pairs, sems)
    stores = []

    def store(at, size):
        part = pl.ds(at, size)
        copy = pltpu.make_async_copy(
            out.at[:, part], out_hbm.at[:, part], sems.at[len(pairs) + len(stores)]
        )
        copy.start()
        stores.append(copy)

    for copy in copies[: n + 1]:
        copy.wait()
    pulled = nt_dot(upstream[...], down[...])
    change = jnp.sum(inner[...].astype(F32) * pulled, axis=1, keepdims=True)
    out[:, 2 * width :] = (change_ref[...] + change).astype(BF16)
    grad_gate = (pulled * to_gate[...]).astype(BF16)
    grad_up = (pulled * to_up[...]).astype(BF16)
    for at in range(0, width, STEP):
        out[:, at : at + STEP] = (
            sum_f[:, at : at + STEP]
            + jnp.dot(act[...], down[:, at : at + STEP], preferred_element_type=F32)
        ).astype(BF16)
    store(0, width)
    for copy in copies[n + 1 :]:
        copy.wait()
    for at in range(0, width, STEP):
        out[:, width + at : width + at + STEP] = (
            sum_b[:, at : at + STEP]
            + jnp.dot(grad_gate, gate[:, at : at + STEP], preferred_element_type=F32)
            + jnp.dot(grad_up, up[:, at : at + STEP], preferred_element_type=F32)
        ).astype(BF16)
    store(width, width + 128)
    for copy in stores:
        copy.wait()


def expert_calls(got, near_pieces, far_pieces, after_near):
    slots = got.shape[0]
    n = 2
    quarter, width = near_pieces[0].shape
    hidden = n * quarter
    full = pltpu.VMEM((hidden, width), BF16)
    vmem = pl.BlockSpec(memory_space=pltpu.VMEM)
    anywhere = pl.BlockSpec(memory_space=pl.ANY)

    def shape(columns, dtype):
        return jax.ShapeDtypeStruct((slots, columns), dtype)

    def params(dots, mib):
        return dict(
            compiler_params=pltpu.CompilerParams(vmem_limit_bytes=mib * MIB),
            cost_estimate=pl.CostEstimate(
                flops=2 * dots * slots * width * hidden,
                bytes_accessed=8 * MIB,
                transcendentals=0,
            ),
        )

    sums = pl.pallas_call(
        functools.partial(near_kernel, n),
        out_shape=[shape(width, F32), shape(width, F32), shape(128, F32)],
        in_specs=[anywhere] + [HBM_SPEC] * 6,
        out_specs=[vmem] * 3,
        scratch_shapes=[pltpu.VMEM((3 * slots, width), BF16), full, full, full]
        + [pltpu.SemaphoreType.DMA((9,))],
        name="near_share",
        **params(8, 32),
    )(got, *near_pieces)
    far_pieces, sums = after_near(far_pieces, sums)
    fronts = pl.pallas_call(
        functools.partial(front_kernel, n),
        out_shape=[
            shape(hidden, BF16),
            shape(hidden, BF16),
            shape(hidden, F32),
            shape(hidden, F32),
        ],
        in_specs=[anywhere] + [HBM_SPEC, anywhere] * 2,
        out_specs=[vmem] * 4,
        scratch_shapes=[pltpu.VMEM((2 * slots, width), BF16), full, full]
        + [pltpu.SemaphoreType.DMA((6,))],
        name="far_front",
        **params(4, 24),
    )(got, *far_pieces[:4])
    return pl.pallas_call(
        functools.partial(far_kernel, n),
        out_shape=pltpu.HBM((slots, 2 * width + 128), BF16),
        in_specs=[anywhere] + [HBM_SPEC, anywhere] * 3 + [vmem] * 7,
        out_specs=HBM_SPEC,
        scratch_shapes=[pltpu.VMEM((slots, width), BF16), full, full, full]
        + [pltpu.VMEM((slots, 2 * width + 128), BF16)]
        + [pltpu.SemaphoreType.DMA((9,))],
        name="far_rest",
        **params(4, 32),
    )(got, *far_pieces, *sums, *fronts)


def end_kernel(
    back_ref, fsel_ref, fcol_ref, sel_ref, col_ref, input_ref, saved_ref, upstream_ref,
    gain_ref, router_ref, mixed_ref, out_ref,
):
    width = saved_ref.shape[1]
    cols = fcol_ref[...]
    back = back_ref[:, :width]
    mixed = cols[:, 0:1] * tn_dot(fsel_ref[0], back)
    mixed = mixed + cols[:, 1:2] * tn_dot(fsel_ref[1], back)
    mixed_ref[...] = (input_ref[...].astype(F32) + mixed).astype(BF16)
    cols = col_ref[...]
    experts = router_ref.shape[0]
    back = back_ref[:, width : 2 * width]
    tail = back_ref[:, 2 * width :]
    change = [
        cols[:, 4 + k : 5 + k] * tn_dot(sel_ref[k], tail)[:, 0:1] for k in range(2)
    ]
    probs = [cols[:, 2 + k : 3 + k] for k in range(2)]
    centre = probs[0] * change[0] + probs[1] * change[1]
    lane = lax.broadcasted_iota(jnp.int32, (cols.shape[0], experts), 1).astype(F32)
    dense = jnp.zeros((cols.shape[0], experts), F32)
    for k in range(2):
        dense = dense + jnp.where(
            lane == cols[:, 6 + k : 7 + k], probs[k] * (change[k] - centre), 0.0
        )
    router_t = router_ref[...]
    total = jnp.zeros((cols.shape[0], width), F32)
    rest = dense
    for _ in range(3):
        term = rest.astype(BF16)
        rest = rest - term.astype(F32)
        total = total + jnp.dot(term, router_t, preferred_element_type=F32)
    for k in range(2):
        total = total + cols[:, k : k + 1] * tn_dot(sel_ref[k], back)
    plain = saved_ref[...].astype(F32)
    inverse = cols[:, 8:9]
    weighted = total * gain_ref[...]
    inner_mean = jnp.mean(weighted * plain, axis=-1, keepdims=True)
    norm_grad = inverse * (weighted - plain * inverse * inverse * inner_mean)
    out_ref[...] = (upstream_ref[...].astype(F32) + norm_grad).astype(BF16)


def end_call(*args):
    like = jax.ShapeDtypeStruct(args[5].shape, BF16)
    vmem = pl.BlockSpec(memory_space=pltpu.VMEM)
    return pl.pallas_call(
        end_kernel,
        out_shape=[like, like],
        in_specs=[vmem] * len(args),
        out_specs=[vmem] * 2,
        compiler_params=pltpu.CompilerParams(vmem_limit_bytes=24 * MIB),
        cost_estimate=pl.CostEstimate(
            flops=8 * args[0].shape[0] * like.shape[0] * like.shape[1],
            bytes_accessed=4 * MIB,
            transcendentals=0,
        ),
        name="finish",
    )(*args)


def trade(rows):
    groups = trade_groups()
    count = len(groups[0])
    blocks = rows.reshape(count, rows.shape[0] // count, rows.shape[1])
    blocks = lax.all_to_all(
        blocks, "expert", 0, 0, axis_index_groups=groups, tiled=True
    )
    return blocks.reshape(rows.shape)


def paired(held, passed):
    return [w for h, p in zip(held, passed) for w in (*in_hbm(h), p)]


def on_device(
    section_input,
    saved_input,
    grad_input,
    expert_ids,
    keep_mask,
    norm_gain,
    router_weight,
    gate_weight,
    up_weight,
    down_weight,
):
    own = (gate_weight[0].T, up_weight[0].T, down_weight[0])
    across, between = z_partners(), core_partners()
    far = [lax.ppermute(w, "expert", across) for w in own]
    near = [lax.ppermute(w, "expert", between) for w in own]
    ids = expert_ids[0].transpose(0, 2, 1)
    keep = keep_mask[0].transpose(0, 2, 1)
    router_t = router_weight[0].T
    slots = router_t.shape[0] * 16
    send, fsel, fcol, bsel, bcol = prologue(
        section_input[0], saved_input[0], grad_input[0], ids, keep, norm_gain, router_t, slots
    )
    send, far[0] = lax.optimization_barrier((send, far[0]))
    near = in_hbm(*near)
    got = trade(send)

    def cross(pieces, sums):
        last, sums = lax.optimization_barrier((pieces[2], sums))
        pieces = [*pieces[:2], last]
        crossed = [lax.ppermute(w, "expert", between) for w in pieces]
        return paired(pieces, crossed), sums

    out = expert_calls(got, paired(own, near), far, cross)
    back = trade(out)
    mixed, input_grad = end_call(
        back, fsel, fcol, bsel, bcol, section_input[0], saved_input[0], grad_input[0], norm_gain, router_t
    )
    return (shifted(mixed[None], 1), shifted(input_grad[None], -1))


def solution(mesh):
    return jax.shard_map(
        on_device,
        mesh=mesh,
        in_specs=(
            P("section", "expert", None),
            P("section", "expert", None),
            P("section", "expert", None),
            P("section", None, "expert", None),
            P("section", None, "expert", None),
            P("section", None),
            P("section", None, None),
            P("section", None, "expert"),
            P("section", None, "expert"),
            P("section", "expert", None),
        ),
        out_specs=(P("section", "expert", None), P("section", "expert", None)),
        check_vma=False,
    )
```

```python
import functools

import jax
import jax.numpy as jnp
from jax import lax
from jax.experimental import pallas as pl
from jax.experimental.pallas import tpu as pltpu
from jax.sharding import PartitionSpec as P

EPS = 1e-06
KEEP_SCALE = 8.0 / 7.0
NEAR_SETS = ((0, 2, 5, 7), (1, 3, 4, 6))
F32 = jnp.float32
BF16 = jnp.bfloat16
MIB = 1 << 20


def place(x, z, core):
    return (x * 8 + z) * 2 + core


def chips():
    return [(x, z, core) for x in range(4) for z in range(8) for core in range(2)]


def trade_groups():
    return [
        [place(x, z, core) for x in range(4) for z in zs]
        for zs in NEAR_SETS
        for core in range(2)
    ]


def z_partners():
    return [(place(x, z, c), place(x, z ^ 1, c)) for x, z, c in chips()]


def core_partners():
    return [(place(x, z, c), place(x, z, c ^ 1)) for x, z, c in chips()]


def shifted(block, distance):
    n = lax.axis_size("section")
    return lax.ppermute(block, "section", [((i - distance) % n, i) for i in range(n)])


def nt_dot(left, right):
    return lax.dot_general(
        left, right, (((1,), (1,)), ((), ())), preferred_element_type=F32
    )


def tn_dot(left, right):
    return lax.dot_general(
        left, right, (((0,), (0,)), ((), ())), preferred_element_type=F32
    )


def whole(shape):
    return pl.BlockSpec(shape, lambda *_: (0,) * len(shape))


def as_column(row):
    n = row.shape[1]
    eye = lax.broadcasted_iota(jnp.int32, (n, n), 0) == lax.broadcasted_iota(
        jnp.int32, (n, n), 1
    )
    return jnp.sum(jnp.where(eye, row, 0.0), axis=1, keepdims=True)


def prepare(hidden, gain, router_t, ids, keep, sel_ref, col_ref):
    tokens = hidden.shape[0]
    experts = router_t.shape[0]
    slots = sel_ref.shape[1]
    per = slots // experts
    plain = hidden.astype(F32)
    inverse = lax.rsqrt(jnp.mean(plain * plain, axis=-1, keepdims=True) + EPS)
    normed = (plain * inverse * gain).astype(BF16)
    logits = nt_dot(router_t, normed)
    expert_row = lax.broadcasted_iota(jnp.int32, (experts, tokens), 0)
    picked = [
        jnp.sum(jnp.where(expert_row == ids[k], logits, 0.0), axis=0, keepdims=True)
        for k in range(2)
    ]
    probs = [1.0 / (1.0 + jnp.exp(picked[1 - k] - picked[k])) for k in range(2)]
    slot = lax.broadcasted_iota(jnp.int32, (slots, tokens), 0)
    slot_expert = slot // per
    slot_rank = slot % per
    named = [slot_expert == ids[k] for k in range(2)]
    named_any = (named[0] | named[1]).astype(F32).astype(BF16)
    earlier = (
        lax.broadcasted_iota(jnp.int32, (tokens, tokens), 0)
        < lax.broadcasted_iota(jnp.int32, (tokens, tokens), 1)
    ).astype(F32).astype(BF16)
    rank = jnp.dot(named_any, earlier, preferred_element_type=F32)
    here = rank == slot_rank.astype(F32)
    sel = [(named[k] & here).astype(F32).astype(BF16) for k in range(2)]
    sel_ref[0] = sel[0]
    sel_ref[1] = sel[1]
    lane = lax.broadcasted_iota(jnp.int32, (tokens, 128), 1)
    kept = [keep[k].astype(F32) * KEEP_SCALE for k in range(2)]
    rows = [
        kept[0] * probs[0],
        kept[1] * probs[1],
        probs[0],
        probs[1],
        kept[0],
        kept[1],
        ids[0].astype(F32),
        ids[1].astype(F32),
    ]
    cols = jnp.zeros((tokens, 128), F32)
    for at, row in enumerate(rows):
        cols = jnp.where(lane == at, as_column(row), cols)
    col_ref[...] = jnp.where(lane == len(rows), inverse, cols)
    return normed, sel[0] + sel[1]


def in_hbm(*arrays):
    return [pltpu.with_memory_space_constraint(a, pltpu.HBM) for a in arrays]


HBM_SPEC = pl.BlockSpec(memory_space=pltpu.HBM)


def start_copies(pairs, sems):
    copies = []
    for at, (source, target) in enumerate(pairs):
        copy = pltpu.make_async_copy(source, target, sems.at[at])
        copy.start()
        copies.append(copy)
    return copies


def prologue_kernel(
    fwd_hbm, bwd_hbm, up_hbm, ids_hbm, keep_hbm, gain_hbm, router_hbm,
    send_hbm, fsel_ref, fcol_ref, bsel_ref, bcol_ref,
    fwd_ref, bwd_ref, up_ref, ids_ref, keep_ref, gain_ref, router_ref, send_ref, sems,
):
    width = fwd_ref.shape[1]
    loads = start_copies(
        [
            (gain_hbm, gain_ref),
            (router_hbm, router_ref),
            (ids_hbm, ids_ref),
            (keep_hbm, keep_ref),
            (fwd_hbm, fwd_ref),
            (bwd_hbm, bwd_ref),
            (up_hbm, up_ref),
        ],
        sems,
    )
    for load in loads[:5]:
        load.wait()
    gain = gain_ref[...]
    router_t = router_ref[...]
    ids = [[ids_ref[m, k : k + 1, :] for k in range(2)] for m in range(2)]
    keep = [[keep_ref[m, k : k + 1, :] for k in range(2)] for m in range(2)]
    stores = []

    experts, per = send_ref.shape[1:3]

    def put(place, sel, values):
        rows = jnp.dot(sel, values, preferred_element_type=F32).astype(BF16)
        send_ref[place] = rows.reshape(experts, per, width)
        store = pltpu.make_async_copy(
            send_ref.at[place],
            send_hbm.at[:, pl.ds(place * per, per), :],
            sems.at[7 + place],
        )
        store.start()
        stores.append(store)

    normed, sel = prepare(fwd_ref[...], gain, router_t, ids[0], keep[0], fsel_ref, fcol_ref)
    put(0, sel, normed)
    loads[5].wait()
    normed, sel = prepare(bwd_ref[...], gain, router_t, ids[1], keep[1], bsel_ref, bcol_ref)
    put(1, sel, normed)
    loads[6].wait()
    put(2, sel, up_ref[...])
    for store in stores:
        store.wait()


def prologue(fwd, bwd, upstream, ids, keep, gain, router_t, slots):
    tokens, width = fwd.shape
    experts = router_t.shape[0]
    per = slots // experts
    sel = jax.ShapeDtypeStruct((2, slots, tokens), BF16)
    col = jax.ShapeDtypeStruct((tokens, 128), F32)
    vmem = pl.BlockSpec(memory_space=pltpu.VMEM)
    args = (fwd, bwd, upstream, ids, keep, gain, router_t)
    return pl.pallas_call(
        prologue_kernel,
        out_shape=(pltpu.HBM((experts, 3 * per, width), BF16), sel, col, sel, col),
        in_specs=[HBM_SPEC] * len(args),
        out_specs=[HBM_SPEC] + [vmem] * 4,
        scratch_shapes=[pltpu.VMEM(a.shape, a.dtype) for a in args]
        + [
            pltpu.VMEM((3, experts, per, width), BF16),
            pltpu.SemaphoreType.DMA((10,)),
        ],
        compiler_params=pltpu.CompilerParams(vmem_limit_bytes=24 * MIB),
        cost_estimate=pl.CostEstimate(
            flops=6 * slots * tokens * width, bytes_accessed=5 * MIB, transcendentals=0
        ),
        name="prologue",
    )(*in_hbm(*args))


def load_pieces(pieces, full, n_pieces):
    quarter = pieces[0].shape[0]
    return [
        (piece, full.at[pl.ds((at % n_pieces) * quarter, quarter)])
        for at, piece in enumerate(pieces)
    ]


def gate_terms(pre_gate, pre_up):
    sigma = jax.nn.sigmoid(pre_gate)
    inner = (pre_gate * sigma * pre_up).astype(BF16)
    to_gate = pre_up * sigma * (1.0 + pre_gate * (1.0 - sigma))
    return inner, to_gate, pre_gate * sigma


STEP = 512


def both_rows(got):
    sources, rows, width = got.shape
    return got[:, : rows * 2 // 3, :].reshape(sources * rows * 2 // 3, width)


def gradient_rows(got):
    sources, rows, width = got.shape
    return got[:, rows * 2 // 3 :, :].reshape(sources * rows // 3, width)


def of_batch(values, m, sources):
    per = values.shape[0] // sources // 2
    split = values.reshape(sources, 2 * per, values.shape[1])
    return split[:, m * per : (m + 1) * per].reshape(sources * per, values.shape[1])


def near_kernel(n, *refs):
    got, pieces, refs = refs[0], refs[1 : 1 + 3 * n], refs[1 + 3 * n :]
    sum_f, sum_b, change_ref, gate, up, down, sems = refs
    width = gate.shape[1]
    sources = got.shape[0]
    pairs = load_pieces(pieces[:n], gate, n)
    pairs += load_pieces(pieces[n : 2 * n], up, n)
    pairs += load_pieces(pieces[2 * n :], down, n)
    copies = start_copies(pairs, sems)
    for copy in copies[:n]:
        copy.wait()
    both = both_rows(got)
    pre_gate = nt_dot(both, gate[...])
    for copy in copies[n : 2 * n]:
        copy.wait()
    pre_up = nt_dot(both, up[...])
    act, _, _ = gate_terms(of_batch(pre_gate, 0, sources), of_batch(pre_up, 0, sources))
    inner, to_gate, to_up = gate_terms(
        of_batch(pre_gate, 1, sources), of_batch(pre_up, 1, sources)
    )
    for copy in copies[2 * n :]:
        copy.wait()
    for at in range(0, width, STEP):
        sum_f[:, at : at + STEP] = jnp.dot(
            act, down[:, at : at + STEP], preferred_element_type=F32
        )
    pulled = nt_dot(gradient_rows(got), down[...])
    change = jnp.sum(inner.astype(F32) * pulled, axis=1, keepdims=True)
    change_ref[...] = jnp.broadcast_to(change, change_ref.shape)
    grad_gate = (pulled * to_gate).astype(BF16)
    grad_up = (pulled * to_up).astype(BF16)
    for at in range(0, width, STEP):
        sum_b[:, at : at + STEP] = jnp.dot(
            grad_gate, gate[:, at : at + STEP], preferred_element_type=F32
        ) + jnp.dot(grad_up, up[:, at : at + STEP], preferred_element_type=F32)


def front_kernel(n, *refs):
    got, pieces, refs = refs[0], refs[1 : 1 + 2 * n], refs[1 + 2 * n :]
    act_ref, inner_ref, to_gate_ref, to_up_ref, gate, up, sems = refs
    sources = got.shape[0]
    both = both_rows(got)
    pairs = load_pieces(pieces[:n], gate, n)
    pairs += load_pieces(pieces[n:], up, n)
    copies = start_copies(pairs, sems)
    for copy in copies[:n]:
        copy.wait()
    pre_gate = nt_dot(both, gate[...])
    for copy in copies[n:]:
        copy.wait()
    pre_up = nt_dot(both, up[...])
    act, _, _ = gate_terms(of_batch(pre_gate, 0, sources), of_batch(pre_up, 0, sources))
    act_ref[...] = act
    inner, to_gate, to_up = gate_terms(
        of_batch(pre_gate, 1, sources), of_batch(pre_up, 1, sources)
    )
    inner_ref[...] = inner
    to_gate_ref[...] = to_gate
    to_up_ref[...] = to_up


def far_kernel(n, *refs):
    got, pieces, refs = refs[0], refs[1 : 1 + 3 * n], refs[1 + 3 * n :]
    sum_f, sum_b, change_ref, act, inner, to_gate, to_up, out_hbm = refs[:8]
    gate, up, down, out, sems = refs[8:]
    width = gate.shape[1]
    pairs = load_pieces(pieces[2 * n :], down, n)
    pairs += load_pieces(pieces[:n], gate, n)
    pairs += load_pieces(pieces[n : 2 * n], up, n)
    copies = start_copies(pairs, sems)
    stores = []

    def store(at, size):
        part = pl.ds(at, size)
        copy = pltpu.make_async_copy(
            out.at[:, part], out_hbm.at[:, part], sems.at[len(pairs) + len(stores)]
        )
        copy.start()
        stores.append(copy)

    for copy in copies[:n]:
        copy.wait()
    pulled = nt_dot(gradient_rows(got), down[...])
    change = jnp.sum(inner[...].astype(F32) * pulled, axis=1, keepdims=True)
    out[:, 2 * width :] = (change_ref[...] + change).astype(BF16)
    grad_gate = (pulled * to_gate[...]).astype(BF16)
    grad_up = (pulled * to_up[...]).astype(BF16)
    for at in range(0, width, STEP):
        out[:, at : at + STEP] = (
            sum_f[:, at : at + STEP]
            + jnp.dot(act[...], down[:, at : at + STEP], preferred_element_type=F32)
        ).astype(BF16)
    store(0, width)
    for copy in copies[n:]:
        copy.wait()
    for at in range(0, width, STEP):
        out[:, width + at : width + at + STEP] = (
            sum_b[:, at : at + STEP]
            + jnp.dot(grad_gate, gate[:, at : at + STEP], preferred_element_type=F32)
            + jnp.dot(grad_up, up[:, at : at + STEP], preferred_element_type=F32)
        ).astype(BF16)
    store(width, width + 128)
    for copy in stores:
        copy.wait()


def expert_calls(got, near_pieces, far_pieces, after_near):
    slots = got.shape[0] * got.shape[1] // 3
    n = 2
    quarter, width = near_pieces[0].shape
    hidden = n * quarter
    full = pltpu.VMEM((hidden, width), BF16)
    vmem = pl.BlockSpec(memory_space=pltpu.VMEM)
    anywhere = pl.BlockSpec(memory_space=pl.ANY)

    def shape(columns, dtype):
        return jax.ShapeDtypeStruct((slots, columns), dtype)

    def params(dots, mib):
        return dict(
            compiler_params=pltpu.CompilerParams(vmem_limit_bytes=mib * MIB),
            cost_estimate=pl.CostEstimate(
                flops=2 * dots * slots * width * hidden,
                bytes_accessed=8 * MIB,
                transcendentals=0,
            ),
        )

    sums = pl.pallas_call(
        functools.partial(near_kernel, n),
        out_shape=[shape(width, F32), shape(width, F32), shape(128, F32)],
        in_specs=[vmem] + [HBM_SPEC] * 6,
        out_specs=[vmem] * 3,
        scratch_shapes=[full, full, full]
        + [pltpu.SemaphoreType.DMA((6,))],
        name="near_share",
        **params(8, 32),
    )(got, *near_pieces)
    far_pieces, sums = after_near(far_pieces, sums)
    fronts = pl.pallas_call(
        functools.partial(front_kernel, n),
        out_shape=[
            shape(hidden, BF16),
            shape(hidden, BF16),
            shape(hidden, F32),
            shape(hidden, F32),
        ],
        in_specs=[vmem] + [HBM_SPEC, anywhere] * 2,
        out_specs=[vmem] * 4,
        scratch_shapes=[full, full]
        + [pltpu.SemaphoreType.DMA((4,))],
        name="far_front",
        **params(4, 24),
    )(got, *far_pieces[:4])
    return pl.pallas_call(
        functools.partial(far_kernel, n),
        out_shape=pltpu.HBM((slots, 2 * width + 128), BF16),
        in_specs=[vmem] + [HBM_SPEC, anywhere] * 3 + [vmem] * 7,
        out_specs=HBM_SPEC,
        scratch_shapes=[full, full, full]
        + [pltpu.VMEM((slots, 2 * width + 128), BF16)]
        + [pltpu.SemaphoreType.DMA((8,))],
        name="far_rest",
        **params(4, 32),
    )(got, *far_pieces, *sums, *fronts)


def end_kernel(
    back_ref, fsel_ref, fcol_ref, sel_ref, col_ref, input_ref, saved_ref, upstream_ref,
    gain_ref, router_ref, mixed_ref, out_ref,
):
    width = saved_ref.shape[1]
    cols = fcol_ref[...]
    back = back_ref[:, :width]
    mixed = cols[:, 0:1] * tn_dot(fsel_ref[0], back)
    mixed = mixed + cols[:, 1:2] * tn_dot(fsel_ref[1], back)
    mixed_ref[...] = (input_ref[...].astype(F32) + mixed).astype(BF16)
    cols = col_ref[...]
    experts = router_ref.shape[0]
    back = back_ref[:, width : 2 * width]
    tail = back_ref[:, 2 * width :]
    change = [
        cols[:, 4 + k : 5 + k] * tn_dot(sel_ref[k], tail)[:, 0:1] for k in range(2)
    ]
    probs = [cols[:, 2 + k : 3 + k] for k in range(2)]
    centre = probs[0] * change[0] + probs[1] * change[1]
    lane = lax.broadcasted_iota(jnp.int32, (cols.shape[0], experts), 1).astype(F32)
    dense = jnp.zeros((cols.shape[0], experts), F32)
    for k in range(2):
        dense = dense + jnp.where(
            lane == cols[:, 6 + k : 7 + k], probs[k] * (change[k] - centre), 0.0
        )
    router_t = router_ref[...]
    total = jnp.zeros((cols.shape[0], width), F32)
    rest = dense
    for _ in range(3):
        term = rest.astype(BF16)
        rest = rest - term.astype(F32)
        total = total + jnp.dot(term, router_t, preferred_element_type=F32)
    for k in range(2):
        total = total + cols[:, k : k + 1] * tn_dot(sel_ref[k], back)
    plain = saved_ref[...].astype(F32)
    inverse = cols[:, 8:9]
    weighted = total * gain_ref[...]
    inner_mean = jnp.mean(weighted * plain, axis=-1, keepdims=True)
    norm_grad = inverse * (weighted - plain * inverse * inverse * inner_mean)
    out_ref[...] = (upstream_ref[...].astype(F32) + norm_grad).astype(BF16)


def end_call(*args):
    like = jax.ShapeDtypeStruct(args[5].shape, BF16)
    vmem = pl.BlockSpec(memory_space=pltpu.VMEM)
    return pl.pallas_call(
        end_kernel,
        out_shape=[like, like],
        in_specs=[vmem] * len(args),
        out_specs=[vmem] * 2,
        compiler_params=pltpu.CompilerParams(vmem_limit_bytes=24 * MIB),
        cost_estimate=pl.CostEstimate(
            flops=8 * args[0].shape[0] * like.shape[0] * like.shape[1],
            bytes_accessed=4 * MIB,
            transcendentals=0,
        ),
        name="finish",
    )(*args)


def trade(blocks):
    return lax.all_to_all(
        blocks, "expert", 0, 0, axis_index_groups=trade_groups(), tiled=True
    )


def paired(held, passed):
    return [w for h, p in zip(held, passed) for w in (*in_hbm(h), p)]


def on_device(
    section_input,
    saved_input,
    grad_input,
    expert_ids,
    keep_mask,
    norm_gain,
    router_weight,
    gate_weight,
    up_weight,
    down_weight,
):
    own = (gate_weight[0].T, up_weight[0].T, down_weight[0])
    across, between = z_partners(), core_partners()
    far = [lax.ppermute(w, "expert", across) for w in own]
    near = [lax.ppermute(w, "expert", between) for w in own]
    ids = expert_ids[0].transpose(0, 2, 1)
    keep = keep_mask[0].transpose(0, 2, 1)
    router_t = router_weight[0].T
    slots = router_t.shape[0] * 16
    send, fsel, fcol, bsel, bcol = prologue(
        section_input[0], saved_input[0], grad_input[0], ids, keep, norm_gain, router_t, slots
    )
    send, far[0] = lax.optimization_barrier((send, far[0]))
    near = in_hbm(*near)
    got = trade(send)

    def cross(pieces, sums):
        last, sums = lax.optimization_barrier((pieces[2], sums))
        pieces = [*pieces[:2], last]
        crossed = [lax.ppermute(w, "expert", between) for w in pieces]
        return paired(pieces, crossed), sums

    out = expert_calls(got, paired(own, near), far, cross)
    back = trade(out.reshape(send.shape[0], -1, out.shape[1])).reshape(out.shape)
    mixed, input_grad = end_call(
        back, fsel, fcol, bsel, bcol, section_input[0], saved_input[0], grad_input[0], norm_gain, router_t
    )
    return (shifted(mixed[None], 1), shifted(input_grad[None], -1))


def solution(mesh):
    return jax.shard_map(
        on_device,
        mesh=mesh,
        in_specs=(
            P("section", "expert", None),
            P("section", "expert", None),
            P("section", "expert", None),
            P("section", None, "expert", None),
            P("section", None, "expert", None),
            P("section", None),
            P("section", None, None),
            P("section", None, "expert"),
            P("section", None, "expert"),
            P("section", "expert", None),
        ),
        out_specs=(P("section", "expert", None), P("section", "expert", None)),
        check_vma=False,
    )
```
